32 devices in a mesh: dp: 16 (over z, y, core), book: 2 (over x).
Axes of the slice: x: 2, y: 2, z: 4, core: 2. Of those that a mesh axis runs over, the one named last changes fastest.
Arguments:
- corpus_rows: bfloat16 [12288, 1024], P('dp'), may hold values from -6 to 6
- code_ids: int32 [12288, 8], P('dp', 'book'), may hold values from 0 to 2047
- master: float32 [8, 2048, 1024], P('book', 'dp'), may hold values from -5 to 5
- first_moment: float32 [8, 2048, 1024], P('book', 'dp'), may hold values from -6 to 6
- second_moment: float32 [8, 2048, 1024], P('book', 'dp'), may hold values from 1 to 30
Outputs:
- new_master: float32 [8, 2048, 1024], P('book', 'dp')
- new_first: float32 [8, 2048, 1024], P('book', 'dp')
- new_second: float32 [8, 2048, 1024], P('book', 'dp')
The draws below stay inside these ranges and needn't reach their ends.
All inputs are finite; a program needn't handle non-finite values.
Results may differ from the reference program's by a relative error of at most 0.002.
Values may be sent and summed in bfloat16 or wider, within the bound.
A program may use at most 192 MiB of HBM per device.

```python
import math
import jax
import jax.numpy as jnp
from jax import lax

D = 1024
K = 2048
M = 8
STEPS = 2
TOKENS = 12288


def with_ends(entries, own_key, least, largest):
    extent = entries.shape
    place = [jax.random.randint(jax.random.fold_in(own_key, axis), (), 0, extent[axis]) for axis in range(len(extent))]
    entries = entries.at[tuple(place)].set(least)
    longest = extent.index(max(extent))
    place[longest] = (place[longest] + 1) % extent[longest]
    return entries.at[tuple(place)].set(largest)


def levels(stream_key, extent, pieces, smallest, top_value):
    level, own = 1.0, jax.random.fold_in(stream_key, 6)
    for axis_at, blocks in pieces:
        steps = jnp.exp(jax.random.uniform(jax.random.fold_in(own, axis_at), (blocks,), jnp.float32, smallest / len(pieces), top_value / len(pieces)))
        level = level * jnp.repeat(steps, extent[axis_at] // blocks).reshape([-1 if axis == axis_at else 1 for axis in range(len(extent))])
    return level


def normal_values(rng, extent, width, bound, split=(), held_as=jnp.bfloat16):
    gain = levels(rng, extent, split, -0.22, 0.18) if split else 1.0
    result = jax.random.normal(rng, extent, jnp.float32) * width * gain
    return jnp.minimum(jnp.maximum(result, -bound), bound).astype(held_as)


def setup_inputs(seed: int = 0) -> dict:
    streams_of = jax.random.split(jax.random.key(seed), 6)
    corpus_rows = normal_values(streams_of[0], (TOKENS, D), 1.0, 6.0, ((0, 16),))
    code_ids = with_ends(jax.random.randint(streams_of[1], (TOKENS, M), 0, K), jax.random.fold_in(streams_of[1], 1), 0, K - 1).astype(jnp.int32)
    master = normal_values(streams_of[2], (M, K, D), 0.35, 5.0, ((0, 2), (1, 16)), jnp.float32)
    first_moment = normal_values(streams_of[3], (M, K, D), 1.0, 6.0, ((0, 2), (1, 16)), jnp.float32)
    second_moment = jnp.clip(jnp.exp(math.log(30.0) - 3.4011974 * jax.random.uniform(streams_of[4], (M, K, D), jnp.float32) ** levels(streams_of[4], (M, K, D), ((0, 2), (1, 16)), -0.2, 0.2)), 1.0, 30.0)
    return dict(corpus_rows=corpus_rows, code_ids=code_ids, master=master, first_moment=first_moment, second_moment=second_moment)


def make_pull(corpus_rows, recon):
    values = corpus_rows.astype(jnp.float32)
    resid = values - recon
    unit = values * lax.rsqrt(lax.optimization_barrier(jnp.sum(values * values, axis=-1, keepdims=True)) + 1e-06)
    along = lax.optimization_barrier(jnp.sum(resid * unit, axis=-1, keepdims=True))
    return (resid + 3.0 * along * unit).astype(jnp.bfloat16)

def reference(corpus_rows, code_ids, master, first_moment, second_moment):
    for turn_index in range(STEPS):
        books = master.astype(jnp.bfloat16)
        recon = jnp.zeros((corpus_rows.shape[0], corpus_rows.shape[1]), jnp.float32)
        for book_slot in range(M):
            recon = recon + jnp.take(books[book_slot], code_ids[:, book_slot], axis=0).astype(jnp.float32)
        pull = make_pull(corpus_rows, recon).astype(jnp.float32)

        def one_book(book_slot):
            ids = jnp.take(code_ids, book_slot, axis=1)
            return -2.0 * jax.ops.segment_sum(pull, ids, num_segments=K)
        grad = lax.map(one_book, jnp.arange(M, dtype=jnp.int32))
        first_moment = 0.9 * first_moment + 0.1 * grad
        second_moment = 0.99 * second_moment + 0.01 * grad * grad
        master = master - 0.05 * first_moment / (jnp.sqrt(second_moment) + 1e-08)
    return (master, first_moment, second_moment)
```

```python
import functools

import jax
import jax.numpy as jnp
from jax import lax
from jax.experimental import pallas as pl
from jax.experimental.pallas import tpu as pltpu
from jax.sharding import PartitionSpec as P

STEPS = 2
LOW = 256
CHUNK = 1024
AXES = ("dp", "book")


def one_hot_of(low_ids, chunk):
    places = lax.broadcasted_iota(jnp.int32, (LOW, chunk), 0)
    return (places == low_ids).astype(jnp.float32).astype(jnp.bfloat16)


def recon_kernel(ids_ref, table_ref, corpus_ref, resid_ref, dots_ref):
    books = ids_ref.shape[0]
    chunk = ids_ref.shape[1]
    cols = corpus_ref.shape[0]
    values = corpus_ref[...].astype(jnp.float32)
    total = jnp.zeros((cols, chunk), jnp.float32)
    for m in range(books):
        ids = ids_ref[m : m + 1, :]
        high = ids // LOW
        picked = jnp.dot(
            table_ref[m], one_hot_of(ids - high * LOW, chunk), preferred_element_type=jnp.float32
        )
        for g in range(table_ref.shape[1] // cols):
            total = total + jnp.where(high == g, picked[g * cols : (g + 1) * cols, :], 0.0)
    resid = values - total
    resid_ref[...] = resid
    dots_ref[0:1, :] = jnp.sum(resid * values, axis=0, keepdims=True)
    dots_ref[1:2, :] = jnp.sum(values * values, axis=0, keepdims=True)


def grad_kernel(ids_ref, resid_ref, corpus_ref, dots_ref, grad_ref):
    books = ids_ref.shape[0]
    chunk = ids_ref.shape[1]
    cols = corpus_ref.shape[0]
    groups = grad_ref.shape[1] // cols

    @pl.when(pl.program_id(0) == 0)
    def _():
        grad_ref[...] = jnp.zeros_like(grad_ref)

    values = corpus_ref[...].astype(jnp.float32)
    scale = lax.rsqrt(dots_ref[1:2, :] + 1e-06)
    along = dots_ref[0:1, :] * scale
    pull = (resid_ref[...] + 3.0 * along * (values * scale)).astype(jnp.bfloat16)
    pull = -2.0 * pull.astype(jnp.float32)
    for m in range(books):
        ids = ids_ref[m : m + 1, :]
        high = ids // LOW
        spread = jnp.concatenate(
            [jnp.where(high == g, pull, 0.0).astype(jnp.bfloat16) for g in range(groups)], axis=0
        )
        grad_ref[m] += lax.dot_general(
            spread,
            one_hot_of(ids - high * LOW, chunk),
            (((1,), (1,)), ((), ())),
            preferred_element_type=jnp.float32,
        )


def run_recon(ids, table, corpus):
    books, tokens = ids.shape
    cols = corpus.shape[0]
    by_token = lambda rows: pl.BlockSpec((rows, CHUNK), lambda i: (0, i))
    whole = pl.BlockSpec(table.shape, lambda i: (0, 0, 0))
    return pl.pallas_call(
        recon_kernel,
        grid=(tokens // CHUNK,),
        in_specs=[by_token(books), whole, by_token(cols)],
        out_specs=[by_token(cols), by_token(2)],
        out_shape=[
            jax.ShapeDtypeStruct((cols, tokens), jnp.float32),
            jax.ShapeDtypeStruct((2, tokens), jnp.float32),
        ],
        compiler_params=pltpu.CompilerParams(vmem_limit_bytes=48 * 2**20),
    )(ids, table, corpus)


def run_grad(ids, resid, corpus, dots, groups):
    books, tokens = ids.shape
    cols = corpus.shape[0]
    by_token = lambda rows: pl.BlockSpec((rows, CHUNK), lambda i: (0, i))
    out = (books, groups * cols, LOW)
    return pl.pallas_call(
        grad_kernel,
        grid=(tokens // CHUNK,),
        in_specs=[by_token(books), by_token(cols), by_token(cols), by_token(2)],
        out_specs=pl.BlockSpec(out, lambda i: (0, 0, 0)),
        out_shape=jax.ShapeDtypeStruct(out, jnp.float32),
        compiler_params=pltpu.CompilerParams(vmem_limit_bytes=48 * 2**20),
    )(ids, resid, corpus, dots)


def per_device(corpus_rows, code_ids, master, first_moment, second_moment):
    local_books, shard, width = master.shape
    local_rows = corpus_rows.shape[0]
    dp, book = lax.axis_size("dp"), lax.axis_size("book")
    devices = dp * book
    cols = width // devices
    padded = max(cols, 16)
    books, codes, tokens = local_books * book, shard * dp, local_rows * dp
    groups = codes // LOW

    def pad_cols(array, axis):
        widths = [(0, 0)] * array.ndim
        widths[axis] = (0, padded - cols)
        return jnp.pad(array, widths) if padded > cols else array

    ids = lax.all_gather(code_ids.T, AXES, axis=0)
    ids = ids.reshape(dp, book, local_books, local_rows).transpose(1, 2, 0, 3).reshape(books, tokens)

    mine = lax.dynamic_index_in_dim(
        corpus_rows.reshape(local_rows, dp, book, cols), lax.axis_index("book"), 2, keepdims=False
    )
    corpus = lax.all_to_all(mine.transpose(1, 2, 0), "dp", 0, 0)
    corpus = pad_cols(corpus.transpose(1, 0, 2).reshape(cols, tokens), 0)

    for _ in range(STEPS):
        outgoing = master.astype(jnp.bfloat16).reshape(local_books, shard, devices, cols)
        incoming = lax.all_to_all(outgoing.transpose(2, 0, 3, 1), AXES, 0, 0)
        table = incoming.reshape(dp, book, local_books, cols, shard).transpose(1, 2, 3, 0, 4)
        table = table.reshape(books, cols, groups, LOW).transpose(0, 2, 1, 3)
        table = pad_cols(table, 2).reshape(books, groups * padded, LOW)
        resid, dots = run_recon(ids, table, corpus)
        dots = lax.psum(dots, AXES)
        grad = run_grad(ids, resid, corpus, dots, groups)
        grad = grad.reshape(books, groups, padded, LOW)[:, :, :cols].transpose(0, 2, 1, 3)
        grad = grad.reshape(book, local_books, cols, dp, shard).transpose(3, 0, 1, 2, 4)
        grad = lax.all_to_all(grad.reshape(devices, local_books, cols, shard), AXES, 0, 0)
        grad = grad.transpose(1, 3, 0, 2).reshape(local_books, shard, width)
        first_moment = 0.9 * first_moment + 0.1 * grad
        second_moment = 0.99 * second_moment + 0.01 * grad * grad
        master = master - 0.05 * first_moment / (jnp.sqrt(second_moment) + 1e-08)
    return (master, first_moment, second_moment)


def solution(mesh):
    state = P("book", "dp", None)
    return jax.shard_map(
        per_device,
        mesh=mesh,
        in_specs=(P("dp", None), P("dp", "book"), state, state, state),
        out_specs=(state, state, state),
        check_vma=False,
    )
```

```python
import functools
import math

import jax
import jax.numpy as jnp
from jax import lax
from jax.experimental import pallas as pl
from jax.experimental.pallas import tpu as pltpu
from jax.sharding import PartitionSpec as P

STEPS = 2
LOW = 256
CHUNK = 1024
PARTS = 1
AXES = ("dp", "book")
VMEM = 48 * 2**20


def one_hot_of(low_ids, chunk):
    places = lax.broadcasted_iota(jnp.int32, (LOW, chunk), 0).astype(jnp.float32).astype(jnp.bfloat16)
    ids = low_ids.astype(jnp.float32).astype(jnp.bfloat16)
    return jnp.where(places == ids, jnp.bfloat16(1), jnp.bfloat16(0))


def recon_kernel(ids_ref, table_ref, corpus_ref, before_ref, resid_ref, dots_ref):
    books = ids_ref.shape[0]
    chunk = ids_ref.shape[1]
    cols = corpus_ref.shape[0]
    total = before_ref[...].astype(jnp.float32)
    for m in range(books):
        ids = ids_ref[m : m + 1, :]
        high = ids // LOW
        picked = jnp.dot(
            table_ref[m], one_hot_of(ids - high * LOW, chunk), preferred_element_type=jnp.float32
        )
        for g in range(table_ref.shape[1] // cols):
            total = total - jnp.where(high == g, picked[g * cols : (g + 1) * cols, :], 0.0)
    resid_ref[...] = total
    values = corpus_ref[...].astype(jnp.float32)
    dots_ref[...] = jnp.sum(total * values, axis=0, keepdims=True)


def grad_kernel(shrink, ids_ref, resid_ref, corpus_ref, coef_ref, out_ref, grad_ref):
    books = ids_ref.shape[0]
    chunk = ids_ref.shape[1]
    cols = corpus_ref.shape[0]
    groups = grad_ref.shape[1] // cols

    @pl.when(pl.program_id(0) == 0)
    def _():
        grad_ref[...] = jnp.zeros_like(grad_ref)

    values = corpus_ref[...].astype(jnp.float32)
    pull = (resid_ref[...] + coef_ref[...] * values).astype(jnp.bfloat16).astype(jnp.float32)
    for m in range(books):
        ids = ids_ref[m : m + 1, :]
        high = ids // LOW
        spread = jnp.concatenate(
            [jnp.where(high == g, pull, 0.0).astype(jnp.bfloat16) for g in range(groups)], axis=0
        )
        grad_ref[m] += lax.dot_general(
            spread,
            one_hot_of(ids - high * LOW, chunk),
            (((1,), (1,)), ((), ())),
            preferred_element_type=jnp.float32,
        )

    @pl.when(pl.program_id(0) == pl.num_programs(0) - 1)
    def _():
        out_ref[...] = (grad_ref[...] * (-2.0 * shrink)).astype(out_ref.dtype)


def adam_kernel(grow, grad_ref, master_ref, first_ref, second_ref, *outs):
    width, shard = master_ref.shape[2], master_ref.shape[1]
    sent = grad_ref[...].astype(jnp.float32).reshape(width, shard) * grow
    grad = sent.T
    first = 0.9 * first_ref[0] + 0.1 * grad
    second = 0.99 * second_ref[0] + 0.01 * grad * grad
    master = master_ref[0] - 0.05 * first / (jnp.sqrt(second) + 1e-08)
    outs[0][0] = master
    outs[1][0] = first
    outs[2][0] = second
    if len(outs) > 3:
        outs[3][...] = master.T.astype(jnp.bfloat16).reshape(outs[3].shape)


def run_recon(ids, table, corpus, before):
    books, tokens = ids.shape
    cols = corpus.shape[0]
    by_token = lambda rows: pl.BlockSpec((rows, CHUNK), lambda i: (0, i))
    whole = pl.BlockSpec(table.shape, lambda i: (0, 0, 0))
    return pl.pallas_call(
        recon_kernel,
        grid=(tokens // CHUNK,),
        in_specs=[by_token(books), whole, by_token(cols), by_token(cols)],
        out_specs=[by_token(cols), by_token(1)],
        out_shape=[
            jax.ShapeDtypeStruct((cols, tokens), jnp.float32),
            jax.ShapeDtypeStruct((1, tokens), jnp.float32),
        ],
        cost_estimate=pl.CostEstimate(
            flops=2 * books * tokens * LOW * table.shape[1], bytes_accessed=10 * cols * tokens, transcendentals=0
        ),
        compiler_params=pltpu.CompilerParams(vmem_limit_bytes=VMEM),
        name="lookup",
    )(ids, table, corpus, before)


def run_grad(ids, resid, corpus, coef, groups, shrink):
    books, tokens = ids.shape
    cols = corpus.shape[0]
    by_token = lambda rows: pl.BlockSpec((rows, CHUNK), lambda i: (0, i))
    out = (books, groups * cols, LOW)
    return pl.pallas_call(
        functools.partial(grad_kernel, shrink),
        grid=(tokens // CHUNK,),
        in_specs=[by_token(books), by_token(cols), by_token(cols), by_token(1)],
        out_specs=pl.BlockSpec(out, lambda i: (0, 0, 0)),
        out_shape=jax.ShapeDtypeStruct(out, jnp.float32),
        scratch_shapes=[pltpu.VMEM(out, jnp.float32)],
        cost_estimate=pl.CostEstimate(
            flops=2 * books * tokens * LOW * groups * cols, bytes_accessed=10 * cols * tokens, transcendentals=0
        ),
        compiler_params=pltpu.CompilerParams(vmem_limit_bytes=VMEM),
        name="scatter",
    )(ids, resid, corpus, coef)


def run_adam(grad, master, first, second, grow, again):
    sources, books, rows, shard = grad.shape
    state = pl.BlockSpec((1,) + master.shape[1:], lambda i: (i, 0, 0))
    moved = pl.BlockSpec((sources, 1, rows, shard), lambda i: (0, i, 0, 0))
    shapes = [jax.ShapeDtypeStruct(master.shape, jnp.float32)] * 3
    specs = [state] * 3
    if again:
        shapes = shapes + [jax.ShapeDtypeStruct(grad.shape, jnp.bfloat16)]
        specs = specs + [moved]
    return pl.pallas_call(
        functools.partial(adam_kernel, grow),
        grid=(books,),
        in_specs=[moved, state, state, state],
        out_specs=specs,
        out_shape=shapes,
        cost_estimate=pl.CostEstimate(
            flops=20 * master.size, bytes_accessed=28 * master.size, transcendentals=master.size
        ),
        compiler_params=pltpu.CompilerParams(vmem_limit_bytes=VMEM),
        name="adam",
    )(grad, master, first, second)


def per_device(corpus_rows, code_ids, master, first_moment, second_moment):
    local_books, shard, width = master.shape
    local_rows = corpus_rows.shape[0]
    dp, book = lax.axis_size("dp"), lax.axis_size("book")
    devices = dp * book
    cols = width // devices
    padded = max(cols, 16)
    parts = PARTS if local_books % PARTS == 0 else 1
    part_books = local_books // parts
    books, codes, tokens = part_books * book, shard * dp, local_rows * dp
    groups = codes // LOW
    bound = 2.0 * tokens * (54.0 + 3.0 * 54.0 * math.sqrt(width))
    shrink = 2.0 ** -max(0, math.ceil(math.log2(bound / 65000.0)))

    def pad_cols(array, axis):
        widths = [(0, 0)] * array.ndim
        widths[axis] = (0, padded - cols)
        return jnp.pad(array, widths) if padded > cols else array

    def to_blocks(moved):
        if cols >= 16:
            return moved
        return moved.transpose(1, 0, 2, 3).reshape(1, moved.shape[1], width, shard)

    def exchange(array):
        return lax.all_to_all(array, AXES, 0, 0)

    def books_out(part):
        cut = part.astype(jnp.bfloat16).reshape(part_books, shard, devices, cols)
        return cut.transpose(2, 0, 3, 1)

    split = lambda array: [array[p * part_books : (p + 1) * part_books] for p in range(parts)]
    masters, firsts, seconds = split(master), split(first_moment), split(second_moment)

    sent_ids = jnp.broadcast_to(code_ids.T.astype(jnp.int16)[None], (devices, local_books, local_rows))
    ids = exchange(sent_ids).astype(jnp.int32)
    ids = ids.reshape(dp, book, parts, part_books, local_rows).transpose(2, 1, 3, 0, 4)
    ids = ids.reshape(parts, books, tokens)

    mine = lax.dynamic_index_in_dim(
        corpus_rows.reshape(local_rows, dp, book, cols), lax.axis_index("book"), 2, keepdims=False
    )
    corpus = lax.all_to_all(mine.transpose(1, 2, 0), "dp", 0, 0)
    corpus = pad_cols(corpus.transpose(1, 0, 2).reshape(cols, tokens), 0)

    values = corpus_rows.astype(jnp.float32)
    squares = jnp.sum(values * values, axis=-1).reshape(book, local_rows // book)
    squares = lax.dynamic_index_in_dim(squares, lax.axis_index("book"), 0, keepdims=False)

    outgoing = [books_out(part) for part in masters]
    for turn in range(STEPS):
        resid = corpus
        for p in range(parts):
            incoming = exchange(outgoing[p])
            table = incoming.reshape(dp, book, part_books, cols, shard).transpose(1, 2, 3, 0, 4)
            table = table.reshape(books, cols, groups, LOW).transpose(0, 2, 1, 3)
            table = pad_cols(table, 2).reshape(books, groups * padded, LOW)
            resid, dots = run_recon(ids[p], table, corpus, resid)
        dots = jnp.sum(exchange(dots.reshape(devices, tokens // devices)), axis=0)
        coef = 3.0 * dots / (squares + 1e-06)
        coef = exchange(jnp.broadcast_to(coef[None], (devices, tokens // devices))).reshape(1, tokens)
        again = turn + 1 < STEPS
        outgoing = []
        for p in range(parts):
            grad = run_grad(ids[p], resid, corpus, coef, groups, shrink)
            grad = grad.reshape(books, groups, padded, LOW)[:, :, :cols].transpose(0, 2, 1, 3).astype(jnp.float16)
            grad = grad.reshape(book, part_books, cols, dp, shard).transpose(3, 0, 1, 2, 4)
            grad = exchange(grad.reshape(devices, part_books, cols, shard))
            out = run_adam(to_blocks(grad).astype(jnp.float32), masters[p], firsts[p], seconds[p], 1.0 / shrink, again)
            masters[p], firsts[p], seconds[p] = out[:3]
            if again:
                moved = out[3]
                if moved.shape[0] != devices:
                    moved = moved.reshape(part_books, devices, cols, shard).transpose(1, 0, 2, 3)
                outgoing.append(moved)
    join = lambda pieces: pieces[0] if parts == 1 else jnp.concatenate(pieces, axis=0)
    return (join(masters), join(firsts), join(seconds))


def solution(mesh):
    state = P("book", "dp", None)
    return jax.shard_map(
        per_device,
        mesh=mesh,
        in_specs=(P("dp", None), P("dp", "book"), state, state, state),
        out_specs=(state, state, state),
        check_vma=False,
    )
```

```python
import functools
import math

import jax
import jax.numpy as jnp
from jax import lax
from jax.experimental import pallas as pl
from jax.experimental.pallas import tpu as pltpu
from jax.sharding import PartitionSpec as P

STEPS = 2
LOW = 256
CHUNK = 1024
PARTS = 1
AXES = ("dp", "book")
VMEM = 48 * 2**20


def one_hot_of(low_ids, chunk):
    places = lax.broadcasted_iota(jnp.int32, (LOW, chunk), 0).astype(jnp.float32).astype(jnp.bfloat16)
    ids = low_ids.astype(jnp.float32).astype(jnp.bfloat16)
    return jnp.where(places == ids, jnp.bfloat16(1), jnp.bfloat16(0))


def recon_kernel(ids_ref, table_ref, corpus_ref, before_ref, resid_ref, dots_ref):
    books = ids_ref.shape[0]
    chunk = ids_ref.shape[1]
    cols = corpus_ref.shape[0]
    total = before_ref[...].astype(jnp.float32)
    for m in range(books):
        ids = ids_ref[m : m + 1, :]
        high = ids // LOW
        picked = jnp.dot(
            table_ref[m], one_hot_of(ids - high * LOW, chunk), preferred_element_type=jnp.float32
        )
        for g in range(table_ref.shape[1] // cols):
            total = total - jnp.where(high == g, picked[g * cols : (g + 1) * cols, :], 0.0)
    resid_ref[...] = total
    values = corpus_ref[...].astype(jnp.float32)
    dots_ref[...] = jnp.sum(total * values, axis=0, keepdims=True)


def grad_kernel(shrink, ids_ref, resid_ref, corpus_ref, coef_ref, out_ref, grad_ref):
    books = ids_ref.shape[0]
    chunk = ids_ref.shape[1]
    cols = corpus_ref.shape[0]
    groups = grad_ref.shape[1] // cols

    @pl.when(pl.program_id(0) == 0)
    def _():
        grad_ref[...] = jnp.zeros_like(grad_ref)

    values = corpus_ref[...].astype(jnp.float32)
    pull = (resid_ref[...] + coef_ref[...] * values).astype(jnp.bfloat16).astype(jnp.float32)
    for m in range(books):
        ids = ids_ref[m : m + 1, :]
        high = ids // LOW
        spread = jnp.concatenate(
            [jnp.where(high == g, pull, 0.0).astype(jnp.bfloat16) for g in range(groups)], axis=0
        )
        grad_ref[m] += lax.dot_general(
            spread,
            one_hot_of(ids - high * LOW, chunk),
            (((1,), (1,)), ((), ())),
            preferred_element_type=jnp.float32,
        )

    @pl.when(pl.program_id(0) == pl.num_programs(0) - 1)
    def _():
        out_ref[...] = (grad_ref[...] * (-2.0 * shrink)).astype(out_ref.dtype)


def adam_kernel(grow, grad_ref, master_ref, first_ref, second_ref, *outs):
    width, shard = master_ref.shape[2], master_ref.shape[1]
    sent = grad_ref[...].reshape(width, shard)
    sent = decode(sent) if sent.dtype == jnp.int16 else sent * grow
    grad = sent.T
    first = 0.9 * first_ref[0] + 0.1 * grad
    second = 0.99 * second_ref[0] + 0.01 * grad * grad
    master = master_ref[0] - 0.05 * first / (jnp.sqrt(second) + 1e-08)
    outs[0][0] = master
    outs[1][0] = first
    outs[2][0] = second
    if len(outs) > 3:
        outs[3][...] = master.T.astype(jnp.bfloat16).reshape(outs[3].shape)


def run_recon(ids, table, corpus, before):
    books, tokens = ids.shape
    cols = corpus.shape[0]
    by_token = lambda rows: pl.BlockSpec((rows, CHUNK), lambda i: (0, i))
    whole = pl.BlockSpec(table.shape, lambda i: (0, 0, 0))
    return pl.pallas_call(
        recon_kernel,
        grid=(tokens // CHUNK,),
        in_specs=[by_token(books), whole, by_token(cols), by_token(cols)],
        out_specs=[by_token(cols), by_token(1)],
        out_shape=[
            jax.ShapeDtypeStruct((cols, tokens), jnp.float32),
            jax.ShapeDtypeStruct((1, tokens), jnp.float32),
        ],
        cost_estimate=pl.CostEstimate(
            flops=2 * books * tokens * LOW * table.shape[1], bytes_accessed=10 * cols * tokens, transcendentals=0
        ),
        compiler_params=pltpu.CompilerParams(vmem_limit_bytes=VMEM),
        name="lookup",
    )(ids, table, corpus, before)


def run_grad(ids, resid, corpus, coef, groups, shrink):
    books, tokens = ids.shape
    cols = corpus.shape[0]
    by_token = lambda rows: pl.BlockSpec((rows, CHUNK), lambda i: (0, i))
    out = (books, groups * cols, LOW)
    return pl.pallas_call(
        functools.partial(grad_kernel, shrink),
        grid=(tokens // CHUNK,),
        in_specs=[by_token(books), by_token(cols), by_token(cols), by_token(1)],
        out_specs=pl.BlockSpec(out, lambda i: (0, 0, 0)),
        out_shape=jax.ShapeDtypeStruct(out, jnp.float32),
        scratch_shapes=[pltpu.VMEM(out, jnp.float32)],
        cost_estimate=pl.CostEstimate(
            flops=2 * books * tokens * LOW * groups * cols, bytes_accessed=10 * cols * tokens, transcendentals=0
        ),
        compiler_params=pltpu.CompilerParams(vmem_limit_bytes=VMEM),
        name="scatter",
    )(ids, resid, corpus, coef)


def run_adam(grad, master, first, second, grow, again):
    sources, books, rows, shard = grad.shape
    state = pl.BlockSpec((1,) + master.shape[1:], lambda i: (i, 0, 0))
    moved = pl.BlockSpec((sources, 1, rows, shard), lambda i: (0, i, 0, 0))
    shapes = [jax.ShapeDtypeStruct(master.shape, jnp.float32)] * 3
    specs = [state] * 3
    if again:
        shapes = shapes + [jax.ShapeDtypeStruct(grad.shape, jnp.bfloat16)]
        specs = specs + [moved]
    return pl.pallas_call(
        functools.partial(adam_kernel, grow),
        grid=(books,),
        in_specs=[moved, state, state, state],
        out_specs=specs,
        out_shape=shapes,
        cost_estimate=pl.CostEstimate(
            flops=20 * master.size, bytes_accessed=28 * master.size, transcendentals=master.size
        ),
        compiler_params=pltpu.CompilerParams(vmem_limit_bytes=VMEM),
        name="adam",
    )(grad, master, first, second)


CODE_GAIN = 900.0
CODE_UNIT = 256.0


def encode(grad):
    level = jnp.log2(1.0 + jnp.abs(grad) * CODE_UNIT) * CODE_GAIN + 0.5
    level = level.astype(jnp.int32)
    return jnp.where(grad < 0.0, -level, level).astype(jnp.int16)


def decode(code):
    level = code.astype(jnp.int32).astype(jnp.float32)
    size = (jnp.exp2(jnp.abs(level) * (1.0 / CODE_GAIN)) - 1.0) * (1.0 / CODE_UNIT)
    return jnp.where(level < 0.0, -size, size)


def step_kernel(
    ids_ref, out_books_ref, corpus_ref, squares_ref, got_ref,
    books_in, table, resid, dots_out, dots_in, coef_out, coef_in, acc, grads_out, grads_in,
    book_send, book_recv, dots_send, dots_recv, coef_send, coef_recv, grad_send, grad_recv,
):
    dp, book = lax.axis_size("dp"), lax.axis_size("book")
    devices = dp * book
    my_d, my_b = lax.axis_index("dp"), lax.axis_index("book")
    me = my_d * book + my_b
    local_books, cols, shard = books_in.shape[1:]
    tokens = ids_ref.shape[1]
    piece = tokens // devices
    chunk = 4 * piece
    chunks = tokens // chunk
    per_low = LOW // shard
    groups = dp // per_low

    def others(body):
        def one(i, carry):
            other = lax.rem(me + i, devices)
            body(other)
            return carry

        lax.fori_loop(1, devices, one, 0)

    def copy_to(source, target, send, recv, d, b):
        return pltpu.make_async_remote_copy(
            src_ref=source, dst_ref=target, send_sem=send, recv_sem=recv,
            device_id=(d, b), device_id_type=pl.DeviceIdType.MESH,
        )

    barrier = pltpu.get_barrier_semaphore()

    def greet(other):
        pl.semaphore_signal(
            barrier, inc=1, device_id=(other // book, lax.rem(other, book)),
            device_id_type=pl.DeviceIdType.MESH,
        )

    others(greet)
    pl.semaphore_wait(barrier, devices - 1)

    def book_copy(slot, other, origin):
        return copy_to(
            out_books_ref.at[other, slot], books_in.at[origin, slot],
            book_send.at[slot, other], book_recv.at[slot, origin], other // book, lax.rem(other, book),
        )

    def send_slot(slot, carry):
        others(lambda other: book_copy(slot, other, me).start())
        return carry

    lax.fori_loop(0, local_books, send_slot, 0)
    books_in[me] = out_books_ref[me]
    resid[...] = corpus_ref[...].astype(jnp.float32)

    def look_up(slot, carry):
        others(lambda other: book_copy(slot, other, other).wait_recv())
        for b in range(book):
            for d in range(dp):
                g, q = d // per_low, d % per_low
                table[b, g * cols : (g + 1) * cols, q * shard : (q + 1) * shard] = books_in[d * book + b, slot]

        def one(c, inner):
            span = pl.ds(pl.multiple_of(c * chunk, chunk), chunk)
            total = resid[:, span]
            for b in range(book):
                ids = ids_ref[pl.ds(b * local_books + slot, 1), span]
                high = ids // LOW
                picked = jnp.dot(
                    table[b], one_hot_of(ids - high * LOW, chunk), preferred_element_type=jnp.float32
                )
                for g in range(groups):
                    total = total - jnp.where(high == g, picked[g * cols : (g + 1) * cols, :], 0.0)
            resid[:, span] = total
            return inner

        lax.fori_loop(0, chunks, one, 0)
        return carry

    lax.fori_loop(0, local_books, look_up, 0)

    def dot_chunk(c, carry):
        span = pl.ds(pl.multiple_of(c * chunk, chunk), chunk)
        dots = jnp.sum(resid[:, span] * corpus_ref[:, span].astype(jnp.float32), axis=0, keepdims=True)
        for i in range(4):
            dots_out[c * 4 + i] = dots[:, i * piece : (i + 1) * piece]
        return carry

    lax.fori_loop(0, chunks, dot_chunk, 0)

    def dot_copy(other, origin):
        return copy_to(
            dots_out.at[other], dots_in.at[origin], dots_send.at[other], dots_recv.at[origin],
            other // book, lax.rem(other, book),
        )

    others(lambda other: dot_copy(other, me).start())
    dots_in[me] = dots_out[me]
    others(lambda other: dot_copy(other, other).wait_recv())
    coef = 3.0 * jnp.sum(dots_in[...], axis=0) / (squares_ref[...] + 1e-06)
    coef_out[...] = coef

    def coef_copy(other, origin):
        return copy_to(
            coef_out, coef_in.at[origin], coef_send.at[other], coef_recv.at[origin],
            other // book, lax.rem(other, book),
        )

    others(lambda other: coef_copy(other, me).start())
    coef_in[me] = coef
    others(lambda other: coef_copy(other, other).wait_recv())

    def pull_chunk(c, carry):
        span = pl.ds(pl.multiple_of(c * chunk, chunk), chunk)
        scale = jnp.concatenate([coef_in[c * 4 + i] for i in range(4)], axis=1)
        pull = resid[:, span] + scale * corpus_ref[:, span].astype(jnp.float32)
        resid[:, span] = pull.astype(jnp.bfloat16).astype(jnp.float32)
        return carry

    lax.fori_loop(0, chunks, pull_chunk, 0)

    def grad_copy(slot, d, b, origin):
        return copy_to(
            grads_out.at[slot, d * book + b], grads_in.at[origin, slot],
            grad_send.at[slot, d * book + b], grad_recv.at[slot, origin], d, b,
        )

    def scatter(turn, carry):
        slot, b = turn // book, lax.rem(turn, book)
        row = pl.ds(b * local_books + slot, 1)
        acc[...] = jnp.zeros_like(acc)

        def one(c, inner):
            span = pl.ds(pl.multiple_of(c * chunk, chunk), chunk)
            ids = ids_ref[row, span]
            high = ids // LOW
            pull = resid[:, span]
            spread = jnp.concatenate(
                [jnp.where(high == g, pull, 0.0).astype(jnp.bfloat16) for g in range(groups)], axis=0
            )
            acc[...] += lax.dot_general(
                spread, one_hot_of(ids - high * LOW, chunk), (((1,), (1,)), ((), ())),
                preferred_element_type=jnp.float32,
            )
            return inner

        lax.fori_loop(0, chunks, one, 0)
        for d in range(dp):
            g, q = d // per_low, d % per_low
            tile = acc[g * cols : (g + 1) * cols, q * shard : (q + 1) * shard]
            grads_out[slot, d * book + b] = encode(-2.0 * tile)

        def send(i, inner):
            d = lax.rem(my_d + i, dp)

            @pl.when(d * book + b != me)
            def _():
                grad_copy(slot, d, b, me).start()

            return inner

        lax.fori_loop(0, dp, send, 0)
        return carry

    lax.fori_loop(0, local_books * book, scatter, 0)

    def finish(slot, carry):
        grads_in[me, slot] = grads_out[slot, me]

        def one(other):
            grad_copy(slot, other // book, lax.rem(other, book), other).wait()
            book_copy(slot, other, me).wait_send()

        others(one)
        return carry

    lax.fori_loop(0, local_books, finish, 0)
    others(lambda other: dot_copy(other, me).wait_send())
    others(lambda other: coef_copy(other, me).wait_send())
    got_ref[...] = grads_in[...]


def run_step(ids, outgoing, corpus, squares):
    devices, local_books, cols, shard = outgoing.shape
    books, tokens = ids.shape
    dp = lax.axis_size("dp")
    piece = tokens // devices
    dma = lambda *shape: pltpu.SemaphoreType.DMA(shape)
    moved = (devices, local_books, cols, shard)
    return pl.pallas_call(
        step_kernel,
        in_specs=[pl.BlockSpec(memory_space=pltpu.VMEM)] * 4,
        out_specs=pl.BlockSpec(memory_space=pltpu.VMEM),
        out_shape=jax.ShapeDtypeStruct(moved, jnp.int16),
        scratch_shapes=[
            pltpu.VMEM(moved, jnp.bfloat16),
            pltpu.VMEM((lax.axis_size("book"), dp * shard // LOW * cols, LOW), jnp.bfloat16),
            pltpu.VMEM((cols, tokens), jnp.float32),
            pltpu.VMEM((devices, 1, piece), jnp.float32),
            pltpu.VMEM((devices, 1, piece), jnp.float32),
            pltpu.VMEM((1, piece), jnp.float32),
            pltpu.VMEM((devices, 1, piece), jnp.float32),
            pltpu.VMEM((dp * shard // LOW * cols, LOW), jnp.float32),
            pltpu.VMEM((local_books, devices, cols, shard), jnp.int16),
            pltpu.VMEM(moved, jnp.int16),
            dma(local_books, devices), dma(local_books, devices),
            dma(devices), dma(devices), dma(devices), dma(devices),
            dma(local_books, devices), dma(local_books, devices),
        ],
        cost_estimate=pl.CostEstimate(
            flops=4 * books * tokens * dp * shard * cols, bytes_accessed=2**23, transcendentals=0
        ),
        compiler_params=pltpu.CompilerParams(
            vmem_limit_bytes=VMEM, collective_id=0, has_side_effects=True
        ),
        name="step",
    )(ids, outgoing, corpus, squares)


def per_device(corpus_rows, code_ids, master, first_moment, second_moment):
    local_books, shard, width = master.shape
    local_rows = corpus_rows.shape[0]
    dp, book = lax.axis_size("dp"), lax.axis_size("book")
    devices = dp * book
    cols = width // devices
    padded = max(cols, 16)
    parts = PARTS if local_books % PARTS == 0 else 1
    part_books = local_books // parts
    books, codes, tokens = part_books * book, shard * dp, local_rows * dp
    groups = codes // LOW
    bound = 2.0 * tokens * (54.0 + 3.0 * 54.0 * math.sqrt(width))
    shrink = 2.0 ** -max(0, math.ceil(math.log2(bound / 65000.0)))

    def pad_cols(array, axis):
        widths = [(0, 0)] * array.ndim
        widths[axis] = (0, padded - cols)
        return jnp.pad(array, widths) if padded > cols else array

    def to_blocks(moved):
        if cols >= 16:
            return moved
        return moved.transpose(1, 0, 2, 3).reshape(1, moved.shape[1], width, shard)

    def exchange(array):
        return lax.all_to_all(array, AXES, 0, 0)

    def books_out(part):
        cut = part.astype(jnp.bfloat16).reshape(part_books, shard, devices, cols)
        return cut.transpose(2, 0, 3, 1)

    split = lambda array: [array[p * part_books : (p + 1) * part_books] for p in range(parts)]
    masters, firsts, seconds = split(master), split(first_moment), split(second_moment)

    sent_ids = jnp.broadcast_to(code_ids.T.astype(jnp.int16)[None], (devices, local_books, local_rows))
    ids = exchange(sent_ids).astype(jnp.int32)
    ids = ids.reshape(dp, book, parts, part_books, local_rows).transpose(2, 1, 3, 0, 4)
    ids = ids.reshape(parts, books, tokens)

    mine = lax.dynamic_index_in_dim(
        corpus_rows.reshape(local_rows, dp, book, cols), lax.axis_index("book"), 2, keepdims=False
    )
    corpus = lax.all_to_all(mine.transpose(1, 2, 0), "dp", 0, 0)
    corpus = pad_cols(corpus.transpose(1, 0, 2).reshape(cols, tokens), 0)

    values = corpus_rows.astype(jnp.float32)
    squares = jnp.sum(values * values, axis=-1).reshape(book, local_rows // book)
    squares = lax.dynamic_index_in_dim(squares, lax.axis_index("book"), 0, keepdims=False)

    outgoing = [books_out(part) for part in masters]
    fused = cols % 16 == 0 and shard % 128 == 0 and LOW % shard == 0 and (tokens // devices) % 128 == 0
    if fused:
        state = (master, first_moment, second_moment)
        outgoing = outgoing[0]
        for turn in range(STEPS):
            codes = run_step(ids[0], outgoing, corpus, squares[None])
            out = run_adam(codes, *state, 1.0, turn + 1 < STEPS)
            state, outgoing = tuple(out[:3]), out[-1]
        return state
    for turn in range(STEPS):
        resid = corpus
        for p in range(parts):
            incoming = exchange(outgoing[p])
            table = incoming.reshape(dp, book, part_books, cols, shard).transpose(1, 2, 3, 0, 4)
            table = table.reshape(books, cols, groups, LOW).transpose(0, 2, 1, 3)
            table = pad_cols(table, 2).reshape(books, groups * padded, LOW)
            resid, dots = run_recon(ids[p], table, corpus, resid)
        dots = jnp.sum(exchange(dots.reshape(devices, tokens // devices)), axis=0)
        coef = 3.0 * dots / (squares + 1e-06)
        coef = exchange(jnp.broadcast_to(coef[None], (devices, tokens // devices))).reshape(1, tokens)
        again = turn + 1 < STEPS
        outgoing = []
        for p in range(parts):
            grad = run_grad(ids[p], resid, corpus, coef, groups, shrink)
            grad = grad.reshape(books, groups, padded, LOW)[:, :, :cols].transpose(0, 2, 1, 3).astype(jnp.float16)
            grad = grad.reshape(book, part_books, cols, dp, shard).transpose(3, 0, 1, 2, 4)
            grad = exchange(grad.reshape(devices, part_books, cols, shard))
            out = run_adam(to_blocks(grad).astype(jnp.float32), masters[p], firsts[p], seconds[p], 1.0 / shrink, again)
            masters[p], firsts[p], seconds[p] = out[:3]
            if again:
                moved = out[3]
                if moved.shape[0] != devices:
                    moved = moved.reshape(part_books, devices, cols, shard).transpose(1, 0, 2, 3)
                outgoing.append(moved)
    join = lambda pieces: pieces[0] if parts == 1 else jnp.concatenate(pieces, axis=0)
    return (join(masters), join(firsts), join(seconds))


def solution(mesh):
    state = P("book", "dp", None)
    return jax.shard_map(
        per_device,
        mesh=mesh,
        in_specs=(P("dp", None), P("dp", "book"), state, state, state),
        out_specs=(state, state, state),
        check_vma=False,
    )
```
